32 devices in a mesh: rep: 2 (over x), tp: 8 (over z, y), sub: 2 (over core).
Axes of the slice: x: 2, y: 2, z: 4, core: 2. Of those that a mesh axis runs over, the one named last changes fastest.
Arguments:
- attn_out: bfloat16 [16, 2, 3, 2048], P('rep', 'sub', None, 'tp'), parts along dimension 0, may hold values from -6 to 6
- w_out: bfloat16 [2048, 16384], P('tp'), may hold values from -0.125 to 0.125
- residual: bfloat16 [96, 16384], P(('rep', 'tp', 'sub')), parts along dimension 0, may hold values from -6 to 6
- norm_gain: float32 [16384], replicated, may hold values from 0.1 to 1.9
- w_query: bfloat16 [16384, 2048], P(None, ('tp', 'sub')), may hold values from -0.046875 to 0.046875
Outputs:
- hidden_out: bfloat16 [96, 16384], P(('rep', 'tp', 'sub')), parts along dimension 0
- query: bfloat16 [96, 2048], P('rep', ('tp', 'sub')), parts along dimension 0
The draws below stay inside these ranges and needn't reach their ends.
There are 2 independent parts, one for each index of `rep`. The reference program is written for one: setup_inputs(seed, part) draws one part's arguments, and reference() takes and returns one part's arrays. A program takes and returns all parts, laid end to end along the dimension named above; an argument that names none is the same for every part. Nothing has to cross between parts.
All inputs are finite; a program needn't handle non-finite values.
Results may differ from the reference program's by a relative error of at most 0.014.
Values may be sent and summed in bfloat16 or wider, within the bound.
A program may use at most 128 MiB of HBM per device.

```python
import jax
import jax.numpy as jnp
from jax import lax

D = 16384
HEAD = 128
BLOCK = 128
TOK_DEV = 3
HEADS = 16
TOKENS = 48
N_TP = 8
N_SUB = 2


def spiked(values, key, source, target, shards_of, factor):
    def block_of(dim):
        return (jnp.arange(values.shape[dim]) // (values.shape[dim] // shards_of)).reshape((-1,) + (1,) * (values.ndim - 1 - dim))

    near = jax.random.permutation(key, shards_of)[block_of(target)]
    other_side = (block_of(target) + shards_of // 2) % shards_of
    return jnp.where((block_of(source) == near) | (block_of(source) == other_side), factor * values, values)


def block_levels(own_key, shape, split, smallest, high):
    def one(dim, blocks):
        heights = jax.random.uniform(jax.random.fold_in(jax.random.fold_in(own_key, 6), dim), (blocks,), jnp.float32, smallest / len(split), high / len(split))
        return jnp.repeat(jnp.exp(heights), shape[dim] // blocks).reshape((-1,) + (1,) * (len(shape) - dim - 1))

    factor_of = one(*split[0])
    for cut in split[1:]:
        factor_of = factor_of * one(*cut)
    return factor_of


def noise(key, shape, deviation, limit, pieces=(), kind=jnp.bfloat16):
    gain = block_levels(key, shape, pieces, -0.22, 0.18) if pieces else 1.0
    values = jax.random.normal(key, shape, jnp.float32) * deviation * gain
    return jnp.minimum(jnp.maximum(values, -limit), limit).astype(kind)


def bell_draw_with(stream_key, dims, deviation, most, pieces, heavy, kind=jnp.bfloat16):
    values = deviation * jax.random.normal(stream_key, dims, jnp.float32)
    if pieces:
        values = values * block_levels(stream_key, dims, pieces, -0.22, 0.18)
    return jnp.clip(spiked(values, jax.random.fold_in(stream_key, 3), *heavy), -most, most).astype(kind)


def setup_inputs(seed: int = 0, part: int = 0) -> dict:
    seeds = jax.random.split(jax.random.key(seed), 6)
    part_keys = jax.random.split(jax.random.fold_in(seeds[5], part), 6)
    attn_out = bell_draw_with(part_keys[0], (N_TP, N_SUB, TOK_DEV, HEADS * HEAD), 1.0, 6.0, ((1, 2), (3, 8)), (3, 0, 8, 2.0))
    w_out = noise(seeds[1], (HEADS * HEAD, D), (HEADS * HEAD) ** -0.5, 0.125, ((0, 8),))
    residual = noise(part_keys[2], (TOKENS, D), 1.0, 6.0, ((0, 16),))
    norm_gain = jnp.clip(1.0 + 0.18 * jax.random.normal(seeds[3], (D,), jnp.float32), 0.1, 1.9)
    w_query = noise(seeds[4], (D, HEADS * HEAD), D ** -0.5, 0.046875, ((1, 16),))
    return dict(attn_out=attn_out, w_out=w_out, residual=residual, norm_gain=norm_gain, w_query=w_query)


def rotation_table(size):
    index = jnp.arange(size, dtype=jnp.int32)
    common = index[:, None] & index[None, :]
    parity = jnp.zeros((size, size), jnp.int32)
    for shift_bit in range(size.bit_length() - 1):
        parity = parity + (common >> shift_bit & 1)
    signs = (1 - 2 * (parity % 2)).astype(jnp.float32)
    return signs / jnp.sqrt(jnp.float32(size))

def rotate(values, rotation):
    blocks = values.reshape(values.shape[0], -1, BLOCK)
    turned = jnp.einsum('tbi,ij->tbj', blocks, rotation, precision=lax.Precision.HIGHEST)
    return turned.reshape(values.shape)

def block_scales(values):
    blocks = values.reshape(values.shape[0], -1, BLOCK)
    return (lax.optimization_barrier(jnp.max(jnp.abs(blocks), axis=-1)) + 1e-06).astype(jnp.bfloat16)

def to_levels(values, scales):
    blocks = values.reshape(values.shape[0], -1, BLOCK)
    levels = (blocks / scales.astype(jnp.float32)[..., None]).astype(jnp.bfloat16)
    return lax.optimization_barrier(levels)

def from_levels(levels, scales):
    return (levels.astype(jnp.float32) * scales.astype(jnp.float32)[..., None]).reshape(levels.shape[0], -1)

def reference(attn_out, w_out, residual, norm_gain, w_query):
    rotation = rotation_table(BLOCK)
    flat = attn_out.reshape(TOKENS, HEADS * HEAD)

    def one_head(head_index, summed):
        start = (head_index * HEAD).astype(jnp.int32)
        inputs = lax.dynamic_slice_in_dim(flat, start, HEAD, 1)
        weights = lax.dynamic_slice_in_dim(w_out, start, HEAD, 0)
        partial_value = rotate(jnp.dot(inputs, weights, preferred_element_type=jnp.float32), rotation)
        scales = block_scales(partial_value)
        levels = to_levels(partial_value, scales)
        return summed + from_levels(levels, scales)
    summed = lax.fori_loop(0, HEADS, one_head, jnp.zeros((TOKENS, D), jnp.float32))
    stream = residual.astype(jnp.float32) + rotate(summed, rotation)
    hidden_out = stream.astype(jnp.bfloat16)
    normed = stream * lax.rsqrt(lax.optimization_barrier(jnp.mean(stream * stream, axis=-1, keepdims=True)) + 1e-05) * norm_gain
    nscale = block_scales(normed)
    nlevel = to_levels(normed, nscale)
    restored = from_levels(nlevel, nscale).astype(jnp.bfloat16)
    query = jnp.dot(restored, w_query, preferred_element_type=jnp.float32).astype(jnp.bfloat16)
    return (hidden_out, query)
```

```python
import functools

import jax
import jax.numpy as jnp
from jax import lax
from jax.experimental import pallas as pl
from jax.experimental.pallas import tpu as pltpu
from jax.sharding import PartitionSpec as P

EPS = 1e-05
LANES = 128
MESH = pl.DeviceIdType.MESH


def kernel(
    outer,
    inner,
    fold,
    a_ref,
    res_ref,
    gain_ref,
    w_hbm,
    wq_hbm,
    hid_ref,
    q_ref,
    w_buf,
    wq_buf,
    part,
    recv1,
    mid,
    recv2,
    gath,
    acc,
    squares,
    w_sem,
    wq_sem,
    send1,
    got1,
    send2,
    got2,
    send_z,
    got_z,
    send_y,
    got_y,
    send_c,
    got_c,
):
    tp = outer * inner
    me = lax.axis_index("tp")
    sub = lax.axis_index("sub")
    zo, yi = me // inner, lax.rem(me, inner)
    toks, tok_local = a_ref.shape[0], res_ref.shape[0]
    cols = part.shape[2]
    width = cols * fold

    def chunk_of(z, y):
        return z * inner + y

    def z_peer(step):
        return lax.rem(zo + step, outer)

    def y_peer(step):
        return lax.rem(yi + step, inner)

    def columns(chunk, f):
        return pl.ds(pl.multiple_of(chunk * width + f * cols, LANES), cols)

    def peer_chunk(m):
        return z_peer(1 + m // (inner - 1)), y_peer(1 + lax.rem(m, inner - 1))

    def w_copy(chunk):
        where = pl.ds(pl.multiple_of(chunk * width, LANES), width)
        return pltpu.make_async_copy(w_hbm.at[:, where], w_buf.at[:, where], w_sem.at[chunk])

    def copy1(z, y):
        return pltpu.make_async_remote_copy(
            part.at[chunk_of(z, y)], recv1.at[yi, z], send1.at[chunk_of(z, y)], got1.at[yi, z],
            device_id={"tp": chunk_of(zo, y)}, device_id_type=MESH,
        )

    def arrive1(y, z):
        return pltpu.make_async_remote_copy(
            recv1.at[y, z], recv1.at[y, z], send1.at[0], got1.at[y, z],
            device_id={"tp": chunk_of(zo, y)}, device_id_type=MESH,
        )

    def copy2(z):
        return pltpu.make_async_remote_copy(
            mid.at[z], recv2.at[zo], send2.at[z], got2.at[zo],
            device_id={"tp": chunk_of(z, yi)}, device_id_type=MESH,
        )

    def arrive2(z):
        return pltpu.make_async_remote_copy(
            recv2.at[z], recv2.at[z], send2.at[0], got2.at[z],
            device_id={"tp": chunk_of(z, yi)}, device_id_type=MESH,
        )

    def spread_z(z):
        return pltpu.make_async_remote_copy(
            gath.at[sub, me], gath.at[sub, me], send_z.at[z], got_z.at[zo],
            device_id={"tp": chunk_of(z, yi)}, device_id_type=MESH,
        )

    def arrive_z(z):
        c = chunk_of(z, yi)
        return pltpu.make_async_remote_copy(
            gath.at[sub, c], gath.at[sub, c], send_z.at[0], got_z.at[z],
            device_id={"tp": c}, device_id_type=MESH,
        )

    def spread_y(z, y):
        c = chunk_of(z, yi)
        return pltpu.make_async_remote_copy(
            gath.at[sub, c], gath.at[sub, c], send_y.at[z, y], got_y.at[c],
            device_id={"tp": chunk_of(zo, y)}, device_id_type=MESH,
        )

    def arrive_y(z, y):
        c = chunk_of(z, y)
        return pltpu.make_async_remote_copy(
            gath.at[sub, c], gath.at[sub, c], send_y.at[0, 0], got_y.at[c],
            device_id={"tp": chunk_of(zo, y)}, device_id_type=MESH,
        )

    def spread_c(c):
        return pltpu.make_async_remote_copy(
            gath.at[sub, c], gath.at[sub, c], send_c.at[c], got_c.at[c],
            device_id={"sub": 1 - sub}, device_id_type=MESH,
        )

    def arrive_c(c):
        return pltpu.make_async_remote_copy(
            gath.at[1 - sub, c], gath.at[1 - sub, c], send_c.at[c], got_c.at[c],
            device_id={"sub": 1 - sub}, device_id_type=MESH,
        )

    def loop(count, body):
        if count <= 8:
            for step in range(count):
                body(step)
        else:
            lax.fori_loop(0, count, lambda i, _: (body(i), None)[1], None)

    peers1 = outer * (inner - 1)

    loop(peers1, lambda m: w_copy(chunk_of(*peer_chunk(m))).start())
    loop(outer, lambda k: w_copy(chunk_of(z_peer(1 + k), yi)).start())
    wq_copy = pltpu.make_async_copy(wq_hbm, wq_buf, wq_sem)
    wq_copy.start()
    barrier = pltpu.get_barrier_semaphore()

    def greet(**where):
        pl.semaphore_signal(barrier, inc=1, device_id=where, device_id_type=MESH)

    loop(outer - 1, lambda k: greet(tp=chunk_of(z_peer(1 + k), yi)))
    loop(inner - 1, lambda k: greet(tp=chunk_of(zo, y_peer(1 + k))))
    greet(sub=1 - sub)

    row = lax.broadcasted_iota(jnp.int32, (toks, cols), 0)

    def partial(chunk):
        w_copy(chunk).wait()
        pieces = []
        for f in range(fold):
            where = columns(chunk, f)
            piece = jnp.dot(a_ref[...], w_buf[:, where], preferred_element_type=jnp.float32)
            mine = res_ref[:, where].astype(jnp.float32)
            for r in range(tok_local):
                piece = piece + jnp.where(row == me * tok_local + r, mine[r : r + 1], 0.0)
            pieces.append(piece)
        return pieces[0] if fold == 1 else jnp.concatenate(pieces, axis=0)

    def first(m, wait_barrier=False):
        z, y = peer_chunk(m)
        part[chunk_of(z, y)] = partial(chunk_of(z, y)).astype(jnp.bfloat16)
        if wait_barrier:
            pl.semaphore_wait(barrier, outer + inner - 1)
        copy1(z, y).start()

    first(0, True)
    loop(peers1 - 1, lambda m: first(m + 1))

    def own(k):
        c = chunk_of(z_peer(1 + k), yi)
        part[c] = partial(c).astype(jnp.bfloat16)

    loop(outer, own)

    def reduced(z):
        total = part[chunk_of(z, yi)].astype(jnp.float32)
        for j in range(1, inner):
            y = y_peer(j)
            arrive1(y, z).wait_recv()
            total = total + recv1[y, z].astype(jnp.float32)
        return total

    def second(k):
        z = z_peer(1 + k)
        mid[z] = reduced(z).astype(jnp.bfloat16)
        copy2(z).start()

    loop(outer - 1, second)
    total = reduced(zo)
    for k in range(1, outer):
        z = z_peer(k)
        arrive2(z).wait_recv()
        total = total + recv2[z].astype(jnp.float32)
    gath[sub, me] = total.astype(jnp.bfloat16)

    loop(outer - 1, lambda k: spread_z(z_peer(1 + k)).start())
    acc[...] = jnp.zeros_like(acc)
    squares[...] = jnp.zeros_like(squares)

    def forward(k):
        z = z_peer(k)
        if not (isinstance(k, int) and k == 0):
            arrive_z(z).wait_recv()
        loop(inner - 1, lambda j: spread_y(z, y_peer(1 + j)).start())
        spread_c(chunk_of(z, yi)).start()

    def hand_over(k):
        z = z_peer(k)

        def one(j):
            y = y_peer(1 + j)
            arrive_y(z, y).wait_recv()
            spread_c(chunk_of(z, y)).start()

        loop(inner - 1, one)

    def use(chunk):
        arrive_c(chunk).wait_recv()
        both = [gath[s, chunk].astype(jnp.float32) for s in range(2)]
        own_rows = gath[sub, chunk].astype(jnp.float32)
        for f in range(fold):
            where = columns(chunk, f)
            span = slice(f * toks, (f + 1) * toks)
            x = jnp.concatenate([both[0][span], both[1][span]], axis=0)
            sq = x * x
            squares[...] += sum(sq[:, j * LANES : (j + 1) * LANES] for j in range(cols // LANES))
            y = (x * gain_ref[:, where]).astype(jnp.bfloat16)
            acc[...] += jnp.dot(y, wq_buf[where, :], preferred_element_type=jnp.float32)
            h = own_rows[span]
            for r in range(tok_local):
                hid_ref[r : r + 1, where] = jnp.sum(
                    jnp.where(row == me * tok_local + r, h, 0.0), axis=0, keepdims=True
                )

    def use_all(k):
        z = z_peer(k)
        loop(inner, lambda j: use(chunk_of(z, y_peer(j))))

    wq_copy.wait()
    forward(0)
    for k in range(1, outer + 2):
        if k < outer:
            forward(k)
        if 1 <= k <= outer:
            hand_over(k - 1)
        if k >= 2:
            use_all(k - 2)

    mean = jnp.sum(squares[...], axis=1, keepdims=True) / (width * tp)
    q_ref[...] = (acc[...] * lax.rsqrt(mean + EPS)).astype(q_ref.dtype)

    def done1(m):
        copy1(*peer_chunk(m)).wait_send()

    loop(peers1, done1)
    loop(outer - 1, lambda k: copy2(z_peer(1 + k)).wait_send())
    loop(outer - 1, lambda k: spread_z(z_peer(1 + k)).wait_send())
    loop(peers1, lambda m: spread_y(peer_chunk(m)[0], peer_chunk(m)[1]).wait_send())
    loop(tp, lambda c: spread_c(c).wait_send())


def shards(attn_out, w_out, residual, norm_gain, w_query):
    tp = lax.axis_size("tp")
    inner = 1
    while (2 * inner) ** 2 <= tp:
        inner *= 2
    outer = tp // inner
    tok_local = residual.shape[0]
    toks = tp * tok_local
    depth, width = w_out.shape
    heads = w_query.shape[1]
    fold = 1 if toks % 16 == 0 else 2
    rows, cols = toks * fold, width // tp // fold
    dma = pltpu.SemaphoreType.DMA
    bf16 = jnp.bfloat16
    vmem = pl.BlockSpec(memory_space=pltpu.VMEM)
    hidden, query = pl.pallas_call(
        functools.partial(kernel, outer, inner, fold),
        out_shape=(
            jax.ShapeDtypeStruct((tok_local, width), jnp.float32),
            jax.ShapeDtypeStruct((2 * toks, heads), jnp.float32),
        ),
        in_specs=[vmem] * 3 + [pl.BlockSpec(memory_space=pl.ANY)] * 2,
        out_specs=(vmem, vmem),
        scratch_shapes=[
            pltpu.VMEM((depth, width), bf16),
            pltpu.VMEM((width, heads), bf16),
            pltpu.VMEM((tp, rows, cols), bf16),
            pltpu.VMEM((inner, outer, rows, cols), bf16),
            pltpu.VMEM((outer, rows, cols), bf16),
            pltpu.VMEM((outer, rows, cols), bf16),
            pltpu.VMEM((2, tp, rows, cols), bf16),
            pltpu.VMEM((2 * toks, heads), jnp.float32),
            pltpu.VMEM((2 * toks, LANES), jnp.float32),
            dma((tp,)),
            dma,
            dma((tp,)),
            dma((inner, outer)),
            dma((outer,)),
            dma((outer,)),
            dma((outer,)),
            dma((outer,)),
            dma((outer, inner)),
            dma((tp,)),
            dma((tp,)),
            dma((tp,)),
        ],
        compiler_params=pltpu.CompilerParams(
            collective_id=0, has_side_effects=True, vmem_limit_bytes=58 * 2**20
        ),
        cost_estimate=pl.CostEstimate(
            flops=2 * toks * depth * width + 4 * toks * width * heads,
            bytes_accessed=2 * (depth + heads) * width,
            transcendentals=0,
        ),
    )(attn_out.reshape(toks, depth), residual, norm_gain.reshape(1, width), w_out, w_query)
    query = query.reshape(2, tp, tok_local, heads).transpose(1, 0, 2, 3).reshape(2 * toks, heads)
    return hidden.astype(bf16), query.astype(bf16)


def solution(mesh):
    placed = (
        P("rep", "sub", None, "tp"),
        P("tp", None),
        P(("rep", "tp", "sub"), None),
        P(),
        P(None, ("tp", "sub")),
    )
    return jax.shard_map(
        shards,
        mesh=mesh,
        in_specs=placed,
        out_specs=(P(("rep", "tp", "sub"), None), P("rep", ("tp", "sub"))),
        check_vma=False,
    )
```

```python
import functools

import jax
import jax.numpy as jnp
from jax import lax
from jax.experimental import pallas as pl
from jax.experimental.pallas import tpu as pltpu
from jax.sharding import PartitionSpec as P

EPS = 1e-05
LANES = 128
SPLIT = 2
MESH = pl.DeviceIdType.MESH


def kernel(
    outer,
    inner,
    fold,
    split,
    a_ref,
    res_ref,
    gain_ref,
    w_hbm,
    wq_hbm,
    hid_ref,
    q_ref,
    w_buf,
    wq_buf,
    part,
    recv1,
    mid,
    recv2,
    gath,
    acc,
    squares,
    q_rows,
    w_sem,
    wq_sem,
    send1,
    got1,
    send2,
    got2,
    send_z,
    got_z,
    send_y,
    got_y,
    send_c,
    got_c,
):
    tp = outer * inner
    me = lax.axis_index("tp")
    sub = lax.axis_index("sub")
    zo, yi = me // inner, lax.rem(me, inner)
    tok_local = res_ref.shape[0]
    toks = tp * tok_local
    cols = part.shape[3]
    piece_width = cols * fold
    width = piece_width * split

    def chunk_of(z, y):
        return z * inner + y

    def z_peer(step):
        return lax.rem(zo + step, outer)

    def y_peer(step):
        return lax.rem(yi + step, inner)

    def columns(chunk, h, f):
        return pl.ds(pl.multiple_of(chunk * width + h * piece_width + f * cols, LANES), cols)

    def peer_chunk(m):
        return z_peer(1 + m // (inner - 1)), y_peer(1 + lax.rem(m, inner - 1))

    def w_copy(chunk, h):
        where = pl.ds(pl.multiple_of(chunk * width + h * piece_width, LANES), piece_width)
        return pltpu.make_async_copy(w_hbm.at[:, where], w_buf.at[:, where], w_sem.at[chunk, h])

    def remote(src, dst, send, got, **where):
        return pltpu.make_async_remote_copy(
            src, dst, send, got, device_id=where, device_id_type=MESH
        )

    def copy1(z, y, h):
        c = chunk_of(z, y)
        return remote(
            part.at[c, h], recv1.at[yi, z, h], send1.at[c, h], got1.at[yi, z, h], tp=chunk_of(zo, y)
        )

    def arrive1(y, z, h):
        slot = recv1.at[y, z, h]
        return remote(slot, slot, send1.at[0, 0], got1.at[y, z, h], tp=chunk_of(zo, y))

    def copy2(z, h):
        return remote(
            mid.at[z, h], recv2.at[zo, h], send2.at[z, h], got2.at[zo, h], tp=chunk_of(z, yi)
        )

    def arrive2(z, h):
        slot = recv2.at[z, h]
        return remote(slot, slot, send2.at[0, 0], got2.at[z, h], tp=chunk_of(z, yi))

    def spread_z(z, h):
        slot = gath.at[sub, me, h]
        return remote(slot, slot, send_z.at[z, h], got_z.at[zo, h], tp=chunk_of(z, yi))

    def arrive_z(z, h):
        c = chunk_of(z, yi)
        slot = gath.at[sub, c, h]
        return remote(slot, slot, send_z.at[0, 0], got_z.at[z, h], tp=c)

    def spread_y(z, y, h):
        c = chunk_of(z, yi)
        slot = gath.at[sub, c, h]
        return remote(slot, slot, send_y.at[z, y, h], got_y.at[c, h], tp=chunk_of(zo, y))

    def arrive_y(z, y, h):
        c = chunk_of(z, y)
        slot = gath.at[sub, c, h]
        return remote(slot, slot, send_y.at[0, 0, 0], got_y.at[c, h], tp=chunk_of(zo, y))

    def spread_c(c, h):
        slot = gath.at[sub, c, h]
        return remote(slot, slot, send_c.at[c, h], got_c.at[c, h], sub=1 - sub)

    def arrive_c(c, h):
        slot = gath.at[1 - sub, c, h]
        return remote(slot, slot, send_c.at[c, h], got_c.at[c, h], sub=1 - sub)

    def loop(count, body):
        if count <= 8:
            for step in range(count):
                body(step)
        else:
            lax.fori_loop(0, count, lambda i, _: (body(i), None)[1], None)

    peers1 = outer * (inner - 1)

    for h in range(split):
        loop(peers1, lambda m: w_copy(chunk_of(*peer_chunk(m)), h).start())
    for h in range(split):
        loop(outer, lambda k: w_copy(chunk_of(z_peer(1 + k), yi), h).start())
    wq_copy = pltpu.make_async_copy(wq_hbm, wq_buf, wq_sem)
    wq_copy.start()
    barrier = pltpu.get_barrier_semaphore()

    def greet(**where):
        pl.semaphore_signal(barrier, inc=1, device_id=where, device_id_type=MESH)

    loop(outer - 1, lambda k: greet(tp=chunk_of(z_peer(1 + k), yi)))
    loop(inner - 1, lambda k: greet(tp=chunk_of(zo, y_peer(1 + k))))
    greet(sub=1 - sub)

    row = lax.broadcasted_iota(jnp.int32, (toks, cols), 0)

    def partial(chunk, h):
        w_copy(chunk, h).wait()
        pieces = []
        for f in range(fold):
            where = columns(chunk, h, f)
            piece = jnp.dot(a_ref[...], w_buf[:, where], preferred_element_type=jnp.float32)
            mine = res_ref[:, where].astype(jnp.float32)
            for r in range(tok_local):
                piece = piece + jnp.where(row == r * tp + me, mine[r : r + 1], 0.0)
            pieces.append(piece)
        return pieces[0] if fold == 1 else jnp.concatenate(pieces, axis=0)

    def first(m, h, wait_barrier=False):
        z, y = peer_chunk(m)
        part[chunk_of(z, y), h] = partial(chunk_of(z, y), h).astype(jnp.bfloat16)
        if wait_barrier:
            pl.semaphore_wait(barrier, outer + inner - 1)
        copy1(z, y, h).start()

    def reduced(z, h):
        total = partial(chunk_of(z, yi), h)
        for j in range(1, inner):
            y = y_peer(j)
            arrive1(y, z, h).wait_recv()
            total = total + recv1[y, z, h].astype(jnp.float32)
        return total

    def second(h):
        def one(k):
            z = z_peer(1 + k)
            mid[z, h] = reduced(z, h).astype(jnp.bfloat16)
            copy2(z, h).start()

        loop(outer - 1, one)

    def third(h):
        total = reduced(zo, h)
        for k in range(1, outer):
            z = z_peer(k)
            arrive2(z, h).wait_recv()
            total = total + recv2[z, h].astype(jnp.float32)
        gath[sub, me, h] = total.astype(jnp.bfloat16)
        loop(outer - 1, lambda k: spread_z(z_peer(1 + k), h).start())
        forward(0, h)

    def forward(k, h):
        z = z_peer(k)
        loop(inner - 1, lambda j: spread_y(z, y_peer(1 + j), h).start())
        spread_c(chunk_of(z, yi), h).start()

    def fourth(h):
        def one(k):
            arrive_z(z_peer(1 + k), h).wait_recv()
            forward(1 + k, h)

        loop(outer - 1, one)

    def fifth(h):
        def one(m):
            z, y = z_peer(m // (inner - 1)), y_peer(1 + lax.rem(m, inner - 1))
            arrive_y(z, y, h).wait_recv()
            spread_c(chunk_of(z, y), h).start()

        loop(peers1, one)

    def use(chunk, h):
        arrive_c(chunk, h).wait_recv()
        both = [gath[s, chunk, h].astype(jnp.float32) for s in range(2)]
        own_rows = gath[sub, chunk, h].astype(jnp.float32)
        for f in range(fold):
            where = columns(chunk, h, f)
            span = slice(f * toks, (f + 1) * toks)
            x = jnp.concatenate([both[0][span], both[1][span]], axis=0)
            sq = x * x
            squares[...] += sum(sq[:, j * LANES : (j + 1) * LANES] for j in range(cols // LANES))
            y = (x * gain_ref[:, where]).astype(jnp.bfloat16)
            acc[...] += jnp.dot(y, wq_buf[where, :], preferred_element_type=jnp.float32)
            h_rows = own_rows[span]
            mine = [
                jnp.sum(jnp.where(row == r * tp + me, h_rows, 0.0), axis=0, keepdims=True)
                for r in range(tok_local)
            ]
            hid_ref[:, where] = jnp.concatenate(mine, axis=0).astype(hid_ref.dtype)

    def sixth(h):
        def one(m):
            use(chunk_of(z_peer(m // inner), y_peer(lax.rem(m, inner))), h)

        loop(tp, one)

    first(0, 0, True)
    loop(peers1 - 1, lambda m: first(m + 1, 0))
    for h in range(1, split):
        loop(peers1, lambda m: first(m, h))
    acc[...] = jnp.zeros_like(acc)
    squares[...] = jnp.zeros_like(squares)
    stages = (second, third, fourth, fifth, sixth)
    for t in range(split + len(stages) - 1):
        if t == len(stages) - 1:
            wq_copy.wait()
        for n, stage in enumerate(stages):
            if 0 <= t - n < split:
                stage(t - n)

    mean = jnp.sum(squares[...], axis=1, keepdims=True) / (width * tp)
    q = acc[...] * lax.rsqrt(mean + EPS)
    for s in range(2):
        for r in range(tok_local):
            start = s * toks + r * tp
            q_rows[pl.ds(s * tok_local + r, tp, stride=2 * tok_local), :] = q[start : start + tp]
    q_ref[...] = q_rows[...].astype(q_ref.dtype)

    for h in range(split):
        loop(peers1, lambda m: copy1(*peer_chunk(m), h).wait_send())
        loop(outer - 1, lambda k: copy2(z_peer(1 + k), h).wait_send())
        loop(outer - 1, lambda k: spread_z(z_peer(1 + k), h).wait_send())
        loop(peers1, lambda m: spread_y(*peer_chunk(m), h).wait_send())
        loop(tp, lambda c: spread_c(c, h).wait_send())


def hand_out(hid_in, q_in, hid_out, q_out):
    hid_out[...] = hid_in[...]
    q_out[...] = q_in[...]


def shards(attn_out, w_out, residual, norm_gain, w_query):
    tp = lax.axis_size("tp")
    inner = 1
    while (2 * inner) ** 2 <= tp:
        inner *= 2
    outer = tp // inner
    tok_local = residual.shape[0]
    toks = tp * tok_local
    depth, width = w_out.shape
    heads = w_query.shape[1]
    fold = 1 if toks % 16 == 0 else 2
    split = max(1, min(SPLIT, width // tp // fold // LANES))
    rows, cols = toks * fold, width // tp // fold // split
    a = attn_out.transpose(1, 2, 0, 3).reshape(toks, depth)
    dma = pltpu.SemaphoreType.DMA
    bf16 = jnp.bfloat16
    vmem = pl.BlockSpec(memory_space=pltpu.VMEM)
    hbm = pl.BlockSpec(memory_space=pl.ANY)
    outs = (
        jax.ShapeDtypeStruct((tok_local, width), bf16),
        jax.ShapeDtypeStruct((2 * toks, heads), bf16),
    )
    results = pl.pallas_call(
        functools.partial(kernel, outer, inner, fold, split),
        out_shape=outs,
        in_specs=[vmem] * 3 + [hbm] * 2,
        out_specs=(vmem, vmem),
        scratch_shapes=[
            pltpu.VMEM((depth, width), bf16),
            pltpu.VMEM((width, heads), bf16),
            pltpu.VMEM((tp, split, rows, cols), bf16),
            pltpu.VMEM((inner, outer, split, rows, cols), bf16),
            pltpu.VMEM((outer, split, rows, cols), bf16),
            pltpu.VMEM((outer, split, rows, cols), bf16),
            pltpu.VMEM((2, tp, split, rows, cols), bf16),
            pltpu.VMEM((2 * toks, heads), jnp.float32),
            pltpu.VMEM((2 * toks, LANES), jnp.float32),
            pltpu.VMEM((2 * toks, heads), jnp.float32),
            dma((tp, split)),
            dma,
            dma((tp, split)),
            dma((inner, outer, split)),
            dma((outer, split)),
            dma((outer, split)),
            dma((outer, split)),
            dma((outer, split)),
            dma((outer, inner, split)),
            dma((tp, split)),
            dma((tp, split)),
            dma((tp, split)),
        ],
        compiler_params=pltpu.CompilerParams(
            collective_id=0, has_side_effects=True, vmem_limit_bytes=58 * 2**20
        ),
        cost_estimate=pl.CostEstimate(
            flops=2 * toks * depth * width + 4 * toks * width * heads,
            bytes_accessed=2 * (depth + heads) * width,
            transcendentals=0,
        ),
    )(a, residual, norm_gain.reshape(1, width), w_out, w_query)
    return pl.pallas_call(hand_out, out_shape=outs, in_specs=[vmem] * 2, out_specs=(vmem, vmem))(
        *results
    )


def solution(mesh):
    placed = (
        P("rep", "sub", None, "tp"),
        P("tp", None),
        P(("rep", "tp", "sub"), None),
        P(),
        P(None, ("tp", "sub")),
    )
    return jax.shard_map(
        shards,
        mesh=mesh,
        in_specs=placed,
        out_specs=(P(("rep", "tp", "sub"), None), P("rep", ("tp", "sub"))),
        check_vma=False,
    )
```

```python
import functools

import jax
import jax.numpy as jnp
from jax import lax
from jax.experimental import pallas as pl
from jax.experimental.pallas import tpu as pltpu
from jax.sharding import PartitionSpec as P

EPS = 1e-05
LANES = 128
SPLIT = 2
MESH = pl.DeviceIdType.MESH


def kernel(
    outer,
    inner,
    fold,
    split,
    a_ref,
    res_ref,
    gain_ref,
    w_hbm,
    wq_hbm,
    hid_ref,
    q_ref,
    w_buf,
    wq_buf,
    part,
    recv1,
    mid,
    recv2,
    gath,
    acc,
    squares,
    q_rows,
    w_sem,
    wq_sem,
    send1,
    got1,
    send2,
    got2,
    send_z,
    got_z,
    send_y,
    got_y,
    send_c,
    got_c,
):
    tp = outer * inner
    me = lax.axis_index("tp")
    sub = lax.axis_index("sub")
    zo, yi = me // inner, lax.rem(me, inner)
    tok_local = res_ref.shape[0]
    toks = tp * tok_local
    cols = part.shape[3]
    piece_width = cols * fold
    width = piece_width * split

    def chunk_of(z, y):
        return z * inner + y

    def z_peer(step):
        return lax.rem(zo + step, outer)

    def z_source(step):
        return lax.rem(zo + outer - step, outer)

    def y_peer(step):
        return lax.rem(yi + step, inner)

    def columns(chunk, h, f):
        return pl.ds(pl.multiple_of(chunk * width + h * piece_width + f * cols, LANES), cols)

    def peer_chunk(m):
        return z_peer(1 + m // (inner - 1)), y_peer(1 + lax.rem(m, inner - 1))

    def w_copy(chunk, h):
        where = pl.ds(pl.multiple_of(chunk * width + h * piece_width, LANES), piece_width)
        return pltpu.make_async_copy(w_hbm.at[:, where], w_buf.at[:, where], w_sem.at[chunk, h])

    def remote(src, dst, send, got, **where):
        return pltpu.make_async_remote_copy(
            src, dst, send, got, device_id=where, device_id_type=MESH
        )

    def copy1(z, y, h):
        c = chunk_of(z, y)
        return remote(
            part.at[c, h], recv1.at[yi, z, h], send1.at[c, h], got1.at[yi, z, h], tp=chunk_of(zo, y)
        )

    def arrive1(y, z, h):
        slot = recv1.at[y, z, h]
        return remote(slot, slot, send1.at[0, 0], got1.at[y, z, h], tp=chunk_of(zo, y))

    def copy2(z, h):
        return remote(
            mid.at[z, h], recv2.at[zo, h], send2.at[z, h], got2.at[zo, h], tp=chunk_of(z, yi)
        )

    def arrive2(z, h):
        slot = recv2.at[z, h]
        return remote(slot, slot, send2.at[0, 0], got2.at[z, h], tp=chunk_of(z, yi))

    def spread_z(z, h):
        slot = gath.at[sub, me, h]
        return remote(slot, slot, send_z.at[z, h], got_z.at[zo, h], tp=chunk_of(z, yi))

    def arrive_z(z, h):
        c = chunk_of(z, yi)
        slot = gath.at[sub, c, h]
        return remote(slot, slot, send_z.at[0, 0], got_z.at[z, h], tp=c)

    def spread_y(z, y, h):
        c = chunk_of(z, yi)
        slot = gath.at[sub, c, h]
        return remote(slot, slot, send_y.at[z, y, h], got_y.at[c, h], tp=chunk_of(zo, y))

    def arrive_y(z, y, h):
        c = chunk_of(z, y)
        slot = gath.at[sub, c, h]
        return remote(slot, slot, send_y.at[0, 0, 0], got_y.at[c, h], tp=chunk_of(zo, y))

    def spread_c(c, h):
        slot = gath.at[sub, c, h]
        return remote(slot, slot, send_c.at[c, h], got_c.at[c, h], sub=1 - sub)

    def arrive_c(c, h):
        slot = gath.at[1 - sub, c, h]
        return remote(slot, slot, send_c.at[c, h], got_c.at[c, h], sub=1 - sub)

    def loop(count, body):
        if count <= 8:
            for step in range(count):
                body(step)
        else:
            lax.fori_loop(0, count, lambda i, _: (body(i), None)[1], None)

    peers1 = outer * (inner - 1)

    for h in range(split):
        loop(peers1, lambda m: w_copy(chunk_of(*peer_chunk(m)), h).start())
    for h in range(split):
        loop(outer, lambda k: w_copy(chunk_of(z_peer(1 + k), yi), h).start())
    wq_copy = pltpu.make_async_copy(wq_hbm, wq_buf, wq_sem)
    wq_copy.start()
    barrier = pltpu.get_barrier_semaphore()

    def greet(**where):
        pl.semaphore_signal(barrier, inc=1, device_id=where, device_id_type=MESH)

    loop(outer - 1, lambda k: greet(tp=chunk_of(z_peer(1 + k), yi)))
    loop(inner - 1, lambda k: greet(tp=chunk_of(zo, y_peer(1 + k))))
    greet(sub=1 - sub)

    row = lax.broadcasted_iota(jnp.int32, (toks, cols), 0)

    def partial(chunk, h):
        w_copy(chunk, h).wait()
        pieces = []
        for f in range(fold):
            where = columns(chunk, h, f)
            piece = jnp.dot(a_ref[...], w_buf[:, where], preferred_element_type=jnp.float32)
            mine = res_ref[:, where].astype(jnp.float32)
            for r in range(tok_local):
                piece = piece + jnp.where(row == r * tp + me, mine[r : r + 1], 0.0)
            pieces.append(piece)
        return pieces[0] if fold == 1 else jnp.concatenate(pieces, axis=0)

    def first(m, h, wait_barrier=False):
        z, y = peer_chunk(m)
        part[chunk_of(z, y), h] = partial(chunk_of(z, y), h).astype(jnp.bfloat16)
        if wait_barrier:
            pl.semaphore_wait(barrier, outer + inner - 1)
        copy1(z, y, h).start()

    def reduced(z, h):
        total = partial(chunk_of(z, yi), h)
        for j in range(1, inner):
            y = y_peer(j)
            arrive1(y, z, h).wait_recv()
            total = total + recv1[y, z, h].astype(jnp.float32)
        return total

    def second(h):
        def one(k):
            z = z_peer(1 + k)
            mid[z, h] = reduced(z, h).astype(jnp.bfloat16)
            copy2(z, h).start()

        loop(outer - 1, one)

    def third(h):
        total = reduced(zo, h)
        for k in range(1, outer):
            z = z_peer(k)
            arrive2(z, h).wait_recv()
            total = total + recv2[z, h].astype(jnp.float32)
        gath[sub, me, h] = total.astype(jnp.bfloat16)
        loop(outer - 1, lambda k: spread_z(z_peer(1 + k), h).start())
        forward(0, h)

    def forward(k, h):
        z = z_source(k)
        loop(inner - 1, lambda j: spread_y(z, y_peer(1 + j), h).start())
        spread_c(chunk_of(z, yi), h).start()

    def fourth(h):
        def one(k):
            arrive_z(z_source(1 + k), h).wait_recv()
            forward(1 + k, h)

        loop(outer - 1, one)

    def use(chunk, h):
        arrive_c(chunk, h).wait_recv()
        both = [gath[s, chunk, h].astype(jnp.float32) for s in range(2)]
        own_rows = gath[sub, chunk, h].astype(jnp.float32)
        for f in range(fold):
            where = columns(chunk, h, f)
            span = slice(f * toks, (f + 1) * toks)
            x = jnp.concatenate([both[0][span], both[1][span]], axis=0)
            sq = x * x
            squares[...] += sum(sq[:, j * LANES : (j + 1) * LANES] for j in range(cols // LANES))
            y = (x * gain_ref[:, where]).astype(jnp.bfloat16)
            acc[...] += jnp.dot(y, wq_buf[where, :], preferred_element_type=jnp.float32)
            h_rows = own_rows[span]
            mine = [
                jnp.sum(jnp.where(row == r * tp + me, h_rows, 0.0), axis=0, keepdims=True)
                for r in range(tok_local)
            ]
            hid_ref[:, where] = jnp.concatenate(mine, axis=0).astype(hid_ref.dtype)

    def use_far(k, h):
        loop(inner - 1, lambda j: use(chunk_of(z_source(k), y_peer(1 + j)), h))

    def fifth(h):
        def one(k):
            z = z_source(k)

            def hand_over(j):
                y = y_peer(1 + j)
                arrive_y(z, y, h).wait_recv()
                spread_c(chunk_of(z, y), h).start()

            if h > 0:
                use_far(k, h - 1)
            use(chunk_of(z, yi), h)
            loop(inner - 1, hand_over)

        loop(outer, one)

    first(0, 0, True)
    loop(peers1 - 1, lambda m: first(m + 1, 0))
    for h in range(1, split):
        loop(peers1, lambda m: first(m, h))
    acc[...] = jnp.zeros_like(acc)
    squares[...] = jnp.zeros_like(squares)
    stages = (second, third, fourth, fifth)
    for t in range(split + len(stages) - 1):
        if t == len(stages) - 1:
            wq_copy.wait()
        for n, stage in enumerate(stages):
            if 0 <= t - n < split:
                stage(t - n)
    loop(outer, lambda k: use_far(k, split - 1))

    mean = jnp.sum(squares[...], axis=1, keepdims=True) / (width * tp)
    q = acc[...] * lax.rsqrt(mean + EPS)
    for s in range(2):
        for r in range(tok_local):
            start = s * toks + r * tp
            q_rows[pl.ds(s * tok_local + r, tp, stride=2 * tok_local), :] = q[start : start + tp]
    q_ref[...] = q_rows[...].astype(q_ref.dtype)

    for h in range(split):
        loop(peers1, lambda m: copy1(*peer_chunk(m), h).wait_send())
        loop(outer - 1, lambda k: copy2(z_peer(1 + k), h).wait_send())
        loop(outer - 1, lambda k: spread_z(z_peer(1 + k), h).wait_send())
        loop(peers1, lambda m: spread_y(*peer_chunk(m), h).wait_send())
        loop(tp, lambda c: spread_c(c, h).wait_send())


def hand_out(hid_in, q_in, hid_out, q_out):
    hid_out[...] = hid_in[...]
    q_out[...] = q_in[...]


def shards(attn_out, w_out, residual, norm_gain, w_query):
    tp = lax.axis_size("tp")
    inner = 1
    while (2 * inner) ** 2 <= tp:
        inner *= 2
    outer = tp // inner
    tok_local = residual.shape[0]
    toks = tp * tok_local
    depth, width = w_out.shape
    heads = w_query.shape[1]
    fold = 1 if toks % 16 == 0 else 2
    split = max(1, min(SPLIT, width // tp // fold // LANES))
    rows, cols = toks * fold, width // tp // fold // split
    a = attn_out.transpose(1, 2, 0, 3).reshape(toks, depth)
    dma = pltpu.SemaphoreType.DMA
    bf16 = jnp.bfloat16
    vmem = pl.BlockSpec(memory_space=pltpu.VMEM)
    hbm = pl.BlockSpec(memory_space=pl.ANY)
    outs = (
        jax.ShapeDtypeStruct((tok_local, width), bf16),
        jax.ShapeDtypeStruct((2 * toks, heads), bf16),
    )
    results = pl.pallas_call(
        functools.partial(kernel, outer, inner, fold, split),
        out_shape=outs,
        in_specs=[vmem] * 3 + [hbm] * 2,
        out_specs=(vmem, vmem),
        scratch_shapes=[
            pltpu.VMEM((depth, width), bf16),
            pltpu.VMEM((width, heads), bf16),
            pltpu.VMEM((tp, split, rows, cols), bf16),
            pltpu.VMEM((inner, outer, split, rows, cols), bf16),
            pltpu.VMEM((outer, split, rows, cols), bf16),
            pltpu.VMEM((outer, split, rows, cols), bf16),
            pltpu.VMEM((2, tp, split, rows, cols), bf16),
            pltpu.VMEM((2 * toks, heads), jnp.float32),
            pltpu.VMEM((2 * toks, LANES), jnp.float32),
            pltpu.VMEM((2 * toks, heads), jnp.float32),
            dma((tp, split)),
            dma,
            dma((tp, split)),
            dma((inner, outer, split)),
            dma((outer, split)),
            dma((outer, split)),
            dma((outer, split)),
            dma((outer, split)),
            dma((outer, inner, split)),
            dma((tp, split)),
            dma((tp, split)),
            dma((tp, split)),
        ],
        compiler_params=pltpu.CompilerParams(
            collective_id=0, has_side_effects=True, vmem_limit_bytes=58 * 2**20
        ),
        cost_estimate=pl.CostEstimate(
            flops=2 * toks * depth * width + 4 * toks * width * heads,
            bytes_accessed=2 * (depth + heads) * width,
            transcendentals=0,
        ),
    )(a, residual, norm_gain.reshape(1, width), w_out, w_query)
    return pl.pallas_call(hand_out, out_shape=outs, in_specs=[vmem] * 2, out_specs=(vmem, vmem))(
        *results
    )


def solution(mesh):
    placed = (
        P("rep", "sub", None, "tp"),
        P("tp", None),
        P(("rep", "tp", "sub"), None),
        P(),
        P(None, ("tp", "sub")),
    )
    return jax.shard_map(
        shards,
        mesh=mesh,
        in_specs=placed,
        out_specs=(P(("rep", "tp", "sub"), None), P("rep", ("tp", "sub"))),
        check_vma=False,
    )
```
